256 devices in a mesh: tile: 64 (over z, x, core), freq: 4 (over y).
Axes of the slice: x: 4, y: 4, z: 8, core: 2. Of those that a mesh axis runs over, the one named last changes fastest.
Arguments:
- u_tiles: bfloat16 [4, 64, 64, 40, 1024], P('freq', 'tile'), may hold values from -0.125 to 0.125
- v_tiles: bfloat16 [4, 64, 64, 40, 1024], P('freq', None, 'tile'), may hold values from -0.1875 to 0.1875
- tile_ranks: int32 [4, 64, 64], P('freq'), may hold values from 4 to 40, as said below
- recorded: float32 [4, 65536, 128], P('freq', 'tile')
Outputs:
- model: float32 [4, 65536, 128], P('freq', 'tile')
- residual: float32 [4, 65536, 128], P('freq', 'tile')
- gradient: float32 [4, 65536, 128], P('freq', 'tile')
The draws below stay inside these ranges and needn't reach their ends.
Inputs may be any that keep to these rules, and one draw needn't show every extreme that they name: `tile_ranks`: every draw holds a tile of rank 40 and a tile of rank 4.
All inputs are finite; a program needn't handle non-finite values.
Results may differ from the reference program's by a relative error of at most 0.02.
Values may be sent and summed in bfloat16 or wider, within the bound.
A program may use at most 128 MiB of HBM per device.

```python
import math
import jax
import jax.numpy as jnp
from jax import lax

TILE_W = 1024
RANK_PAD = 40
TRACES = 128
ITERS = 2
TILES = 64
FREQS = 4


def draw_tile_ranks(key, part):
    first, second, third = jax.random.split(jax.random.fold_in(key, 11), 3)
    shape = (FREQS, TILES, TILES)
    left = jax.random.randint(first, shape, 0, RANK_PAD - 3)
    right = jax.random.randint(second, shape, 0, RANK_PAD - 3)
    divisor = max((RANK_PAD - 4) * 18 // 25, 1)
    ranks_all = jnp.minimum(4 + left * right // divisor, RANK_PAD)
    flat = ranks_all.reshape(-1)
    total = FREQS * TILES * TILES
    spot = jax.random.randint(third, (), 0, total)
    flat = flat.at[spot].set(RANK_PAD)
    flat = flat.at[(spot + 1) % total].set(4)
    return flat.reshape(shape).astype(jnp.int32)


def draw_recorded(key, part):
    first, second = jax.random.split(jax.random.fold_in(key, 23), 2)
    shape = (FREQS, TILES * TILE_W, TRACES)
    tile_of_row = (jnp.arange(TILES * TILE_W) // TILE_W).astype(jnp.float32)
    block_scale = 1.0 + 2.0 * tile_of_row / max(TILES - 1, 1)
    row_scale = jnp.exp(jax.random.uniform(second, (FREQS, TILES * TILE_W, 1), jnp.float32, 0.0, math.log(10.0)))
    base = jax.random.normal(first, shape, jnp.float32)
    return (block_scale[None, :, None] * row_scale * base).astype(jnp.float32)


def steps_of(stream_key, dims, shards, smallest, high):
    def one(axis_at, shards_of):
        heights = jax.random.uniform(jax.random.fold_in(jax.random.fold_in(stream_key, 6), axis_at), (shards_of,), jnp.float32, smallest / len(shards), high / len(shards))
        return jnp.repeat(jnp.exp(heights), dims[axis_at] // shards_of).reshape((-1,) + (1,) * (len(dims) - axis_at - 1))

    loudness = one(*shards[0])
    for cut in shards[1:]:
        loudness = loudness * one(*cut)
    return loudness


def centred(own_key, shape, spread, limit, cuts=(), held_as=jnp.bfloat16):
    drawn = spread * jax.random.normal(own_key, shape, jnp.float32)
    if cuts:
        drawn = drawn * steps_of(own_key, shape, cuts, -0.22, 0.18)
    return jnp.clip(drawn, -limit, limit).astype(held_as)


def setup_inputs(seed: int = 0) -> dict:
    seeds = jax.random.split(jax.random.key(seed), 5)
    return {
        "u_tiles": centred(seeds[0], (FREQS, TILES, TILES, RANK_PAD, TILE_W), (TILES * RANK_PAD) ** -0.5, 0.125, ((0, 4), (1, 64))),
        "v_tiles": centred(seeds[1], (FREQS, TILES, TILES, RANK_PAD, TILE_W), TILE_W ** -0.5, 0.1875, ((0, 4), (2, 64))),
        "tile_ranks": draw_tile_ranks(jax.random.fold_in(seeds[4], 71), 0),
        "recorded": draw_recorded(jax.random.fold_in(seeds[4], 71), 0),
    }


def rank_levels(tile_ranks):
    levels = jnp.arange(RANK_PAD, dtype=jnp.int32)
    return (levels < tile_ranks[..., None]).astype(jnp.float32)


def to_wire(value):
    return lax.optimization_barrier(value.astype(jnp.bfloat16)).astype(jnp.float32)


def forward_one(u_freq, v_freq, mask_freq, direction):
    rounded = to_wire(direction).reshape(TILES, TILE_W, TRACES)

    def tile_row(pieces):
        u_row, v_row, mask_row = pieces
        coeffs = jnp.einsum("jrb,jbs->jrs", v_row.astype(jnp.float32), rounded) * mask_row[:, :, None]
        coeffs = to_wire(coeffs)
        return jnp.einsum("jrb,jrs->bs", u_row.astype(jnp.float32), coeffs)

    return lax.map(tile_row, (u_freq, v_freq, mask_freq)).reshape(TILES * TILE_W, TRACES)


def adjoint_one(u_freq, v_freq, mask_freq, resid):
    rounded = to_wire(resid).reshape(TILES, TILE_W, TRACES)

    def tile_row(total, pieces):
        u_row, v_row, mask_row, r_row = pieces
        coeffs = jnp.einsum("jrb,bs->jrs", u_row.astype(jnp.float32), r_row) * mask_row[:, :, None]
        coeffs = to_wire(coeffs)
        return total + jnp.einsum("jrb,jrs->jbs", v_row.astype(jnp.float32), coeffs), None

    start = jnp.zeros((TILES, TILE_W, TRACES), jnp.float32)
    total, unused = lax.scan(tile_row, start, (u_freq, v_freq, mask_freq, rounded))
    return total.reshape(TILES * TILE_W, TRACES)


def reference(u_tiles, v_tiles, tile_ranks, recorded):
    masks = rank_levels(tile_ranks)

    def forward(field):
        return jnp.stack([forward_one(u_tiles[f], v_tiles[f], masks[f], field[f]) for f in range(FREQS)])

    def adjoint(field):
        return jnp.stack([adjoint_one(u_tiles[f], v_tiles[f], masks[f], field[f]) for f in range(FREQS)])

    model = jnp.zeros_like(recorded)
    resid = recorded
    gradient = adjoint(resid)
    direction = gradient
    gamma = jnp.sum(gradient * gradient)
    for iteration in range(ITERS):
        image = forward(direction)
        delta = jnp.sum(image * image)
        alpha = gamma / delta
        model = model + alpha * direction
        resid = resid - alpha * image
        gradient = adjoint(resid)
        gamma_new = jnp.sum(gradient * gradient)
        direction = gradient + (gamma_new / gamma) * direction
        gamma = gamma_new
    return model, resid, gradient
```

```python
import jax
import jax.numpy as jnp
from jax import lax
from jax.experimental import pallas as pl
from jax.experimental.pallas import tpu as pltpu
from jax.sharding import Mesh
from jax.sharding import PartitionSpec as P

MESH = pl.DeviceIdType.MESH
NZ, NX, NC, NF = 8, 4, 2, 4
RANK, WIDTH, TRACES = 40, 1024, 128
PLANE = NX * NC
GROUP = PLANE * RANK
TILES = NZ * PLANE
APPS = 5
PLANE_ORDER = ((2, 1), (2, 0), (1, 1), (3, 1), (1, 0), (3, 0), (0, 1), (0, 0))


def kernel(
    u_hbm, v_hbm, ranks, recorded,
    model_out, resid_out, grad_out,
    w, field, total, resid, grad, image, direc,
    sent, held, red_a, red_b, red_c,
    load_sem, send_sem, recv_sem, own_sem,
    red_send, red_recv,
):
    z, x, c = lax.axis_index("z"), lax.axis_index("x"), lax.axis_index("c")
    freq = lax.axis_index("freq")
    place = x * NC + c
    me = z * PLANE + place

    def at(dz, dx, dc):
        return {"z": lax.rem(z + dz, NZ), "x": lax.rem(x + dx, NX), "c": lax.rem(c + dc, NC)}

    def at_freq(df):
        return {"freq": lax.rem(freq + df, NF)}

    loads = [
        pltpu.make_async_copy(hbm, w.at[k], load_sem.at[k]) for k, hbm in enumerate((u_hbm, v_hbm))
    ]
    for load in loads:
        load.start()

    barrier = pltpu.get_barrier_semaphore()

    def greet(dz, carry):
        for dx, dc in PLANE_ORDER[:-1]:
            pl.semaphore_signal(barrier, 1, device_id=at(dz, dx, dc), device_id_type=MESH)
        return carry

    def greet_z(dz, carry):
        pl.semaphore_signal(barrier, 1, device_id=at(dz, 0, 0), device_id_type=MESH)
        return carry

    lax.fori_loop(0, NZ, greet, 0)
    lax.fori_loop(1, NZ, greet_z, 0)
    for df in range(1, NF):
        pl.semaphore_signal(barrier, 1, device_id=at_freq(df), device_id_type=MESH)

    resid[...] = recorded[...].T
    field[...] = resid[...].astype(jnp.bfloat16)
    level = lax.broadcasted_iota(jnp.int32, (RANK, TRACES), 0)

    def partial_squares(value):
        return jnp.sum((value * value).reshape(TRACES // 8, 8, WIDTH // 128, 128), axis=(0, 2))

    def spread(s, which, count, slot, targets):
        buffer = (red_a, red_b, red_c)[which]
        for target in targets:
            pltpu.make_async_remote_copy(
                src_ref=buffer.at[s, slot],
                dst_ref=buffer.at[s, slot],
                send_sem=red_send.at[s, which],
                recv_sem=red_recv.at[s, which],
                device_id=target,
                device_id_type=MESH,
            ).start()

    def collect(s, which, count):
        buffer = (red_a, red_b, red_c)[which]
        several = buffer.at[s, pl.ds(0, count - 1)]
        pltpu.make_async_copy(several, several, red_recv.at[s, which]).wait()
        pltpu.make_async_copy(several, several, red_send.at[s, which]).wait()
        return jnp.sum(buffer[s], axis=0)

    def sum_first(s, value):
        red_a[s, place] = partial_squares(value)
        spread(s, 0, PLANE, place, [at(0, dx, dc) for dx, dc in PLANE_ORDER[:-1]])

    def sum_second(s):
        red_b[s, z] = collect(s, 0, PLANE)
        spread(s, 1, NZ, z, [at(dz, 0, 0) for dz in range(1, NZ)])

    def sum_third(s):
        red_c[s, freq] = collect(s, 1, NZ)
        spread(s, 2, NF, freq, [at_freq(df) for df in range(1, NF)])

    def sum_last(s):
        return jnp.sum(collect(s, 2, NF), keepdims=True)

    def apply(app, after_first=None, after_sends=None, middle=None, late=None):
        first = app % 2

        def offset_of(step):
            half = (step + 1) // 2
            odd = lax.rem(step, 2)
            return lax.rem(NZ // 2 + NZ + (1 - 2 * odd) * half, NZ)

        def coefficients(zone):
            start = pl.multiple_of(zone * GROUP, GROUP)
            value = lax.dot_general(
                w[first, pl.ds(start, GROUP), :],
                field[...],
                (((1,), (1,)), ((), ())),
                preferred_element_type=jnp.float32,
            )
            for t in range(PLANE):
                tile = zone * PLANE + t
                rank = ranks[me, tile] if first == 0 else ranks[tile, me]
                part = value[t * RANK : (t + 1) * RANK]
                sent[app, tile] = jnp.where(level < rank, part, 0.0).astype(jnp.bfloat16)

        def send(dz, dx, dc):
            zone = lax.rem(z + dz, NZ)
            tile = zone * PLANE + lax.rem(x + dx, NX) * NC + lax.rem(c + dc, NC)
            pltpu.make_async_remote_copy(
                src_ref=sent.at[app, tile],
                dst_ref=held.at[app, me],
                send_sem=send_sem.at[app],
                recv_sem=recv_sem.at[app, z],
                device_id=at(dz, dx, dc),
                device_id_type=MESH,
            ).start()

        def send_zone(step, carry):
            dz = offset_of(step)
            coefficients(lax.rem(z + dz, NZ))
            if app == 0:
                pl.when(step == 0)(lambda: pl.semaphore_wait(barrier, TILES - 1 + NF - 1))
            for dx, dc in PLANE_ORDER:
                send(dz, dx, dc)
            return carry

        lax.fori_loop(0, NZ - 1, send_zone, 0)
        coefficients(z)
        for dx, dc in PLANE_ORDER[:-1]:
            send(0, dx, dc)
        own = pltpu.make_async_copy(sent.at[app, me], held.at[app, me], own_sem.at[app])
        own.start()
        if after_sends is not None:
            after_sends()

        total[...] = jnp.zeros_like(total)

        def take(zone):
            start = pl.multiple_of(zone * PLANE, PLANE)
            value = held[app, pl.ds(start, PLANE)].astype(jnp.float32)
            value = value.reshape(GROUP, TRACES).T.astype(jnp.bfloat16)
            rows = pl.multiple_of(zone * GROUP, GROUP)
            total[...] += lax.dot_general(
                value,
                w[1 - first, pl.ds(rows, GROUP), :],
                (((1,), (0,)), ((), ())),
                preferred_element_type=jnp.float32,
            )

        def take_zone(step, carry):
            zone = lax.rem(z - offset_of(step) + NZ, NZ)
            start = pl.multiple_of(zone * PLANE, PLANE)
            group = held.at[app, pl.ds(start, PLANE)]
            pltpu.make_async_copy(group, group, recv_sem.at[app, zone]).wait()
            take(zone)
            return carry

        lax.fori_loop(0, 4, take_zone, 0)
        if middle is not None:
            middle()
        lax.fori_loop(4, NZ - 1, take_zone, 0)
        if late is not None:
            late()
        several = held.at[app, pl.ds(0, PLANE - 1)]
        pltpu.make_async_copy(several, several, recv_sem.at[app, z]).wait()
        own.wait()
        take(z)

    loads[0].wait()
    loads[1].wait()
    apply(0)
    grad[...] = total[...]
    field[...] = grad[...].astype(jnp.bfloat16)
    sum_first(0, grad[...])
    apply(1, after_sends=lambda: sum_second(0), middle=lambda: sum_third(0))
    image[...] = total[...]
    field[...] = image[...].astype(jnp.bfloat16)
    sum_first(1, image[...])
    gamma = sum_last(0)
    apply(2, after_sends=lambda: sum_second(1), middle=lambda: sum_third(1))
    delta = sum_last(1)
    alpha = gamma / delta
    direc[...] = grad[...]
    grad[...] = grad[...] - alpha * total[...]
    field[...] = grad[...].astype(jnp.bfloat16)
    sum_first(2, grad[...])
    resid[...] = resid[...] - alpha * image[...]
    apply(3, after_sends=lambda: sum_second(2), middle=lambda: sum_third(2))
    gamma_new = sum_last(2)
    beta = gamma_new / gamma
    image[...] = total[...] + beta * image[...]
    field[...] = image[...].astype(jnp.bfloat16)
    sum_first(3, image[...])

    def finish():
        scale = gamma_new / sum_last(3)
        old = direc[...]
        model_out[...] = (alpha * old + scale * (grad[...] + beta * old)).T
        resid_out[...] = (resid[...] - scale * image[...]).T
        direc[0:1, 0:128] = jnp.broadcast_to(scale, (1, 128))

    apply(4, after_sends=lambda: sum_second(3), middle=lambda: sum_third(3), late=finish)
    grad_out[...] = (grad[...] - direc[0:1, 0:1] * total[...]).T

    for app in range(APPS):
        several = sent.at[app, pl.ds(0, TILES - 1)]
        pltpu.make_async_copy(several, several, send_sem.at[app]).wait()


def local(u_tiles, v_tiles, tile_ranks, recorded):
    rows = TILES * RANK
    field = jax.ShapeDtypeStruct((WIDTH, TRACES), jnp.float32)
    flat = pltpu.VMEM((TRACES, WIDTH), jnp.float32)
    vmem = pl.BlockSpec(memory_space=pltpu.VMEM)
    outs = pl.pallas_call(
        kernel,
        out_shape=(field,) * 3,
        in_specs=[
            pl.BlockSpec(memory_space=pl.ANY),
            pl.BlockSpec(memory_space=pl.ANY),
            pl.BlockSpec(memory_space=pltpu.SMEM),
            vmem,
        ],
        out_specs=(vmem,) * 3,
        scratch_shapes=[
            pltpu.VMEM((2, rows, WIDTH), jnp.bfloat16),
            pltpu.VMEM((TRACES, WIDTH), jnp.bfloat16),
            flat, flat, flat, flat, flat,
            pltpu.VMEM((APPS, TILES, RANK, TRACES), jnp.bfloat16),
            pltpu.VMEM((APPS, TILES, RANK, TRACES), jnp.bfloat16),
            pltpu.VMEM((4, PLANE, 8, 128), jnp.float32),
            pltpu.VMEM((4, NZ, 8, 128), jnp.float32),
            pltpu.VMEM((4, NF, 8, 128), jnp.float32),
            pltpu.SemaphoreType.DMA((2,)),
            pltpu.SemaphoreType.DMA((APPS,)),
            pltpu.SemaphoreType.DMA((APPS, NZ)),
            pltpu.SemaphoreType.DMA((APPS,)),
            pltpu.SemaphoreType.DMA((4, 3)),
            pltpu.SemaphoreType.DMA((4, 3)),
        ],
        compiler_params=pltpu.CompilerParams(
            collective_id=0, has_side_effects=True, vmem_limit_bytes=48 << 20
        ),
        cost_estimate=pl.CostEstimate(
            flops=APPS * 4 * rows * WIDTH * TRACES, bytes_accessed=12 << 20, transcendentals=0
        ),
    )(
        u_tiles.reshape(rows, WIDTH),
        v_tiles.reshape(rows, WIDTH),
        tile_ranks.reshape(TILES, TILES),
        recorded.reshape(WIDTH, TRACES),
    )
    return tuple(out.reshape(1, WIDTH, TRACES) for out in outs)


def solution(mesh):
    torus = Mesh(mesh.devices.reshape(NZ, NX, NC, NF), ("z", "x", "c", "freq"))
    tile = ("z", "x", "c")
    in_specs = (
        P("freq", tile, None, None, None),
        P("freq", None, tile, None, None),
        P("freq", None, None),
        P("freq", tile, None),
    )
    out_specs = (P("freq", tile, None),) * 3
    return jax.shard_map(local, mesh=torus, in_specs=in_specs, out_specs=out_specs, check_vma=False)
```

```python
import jax
import jax.numpy as jnp
from jax import lax
from jax.experimental import pallas as pl
from jax.experimental.pallas import tpu as pltpu
from jax.sharding import Mesh
from jax.sharding import PartitionSpec as P

MESH = pl.DeviceIdType.MESH
NZ, NX, NC, NF = 8, 4, 2, 4
RANK, WIDTH, TRACES = 40, 1024, 128
PLANE = NX * NC
GROUP = NZ * RANK
TILES = NZ * PLANE
APPS = 5
PLANE_ORDER = ((2, 1), (2, 0), (1, 1), (3, 1), (1, 0), (3, 0), (0, 1), (0, 0))
ZONE_ORDER = (4, 3, 5, 2, 6, 1, 7, 0)


def kernel(
    u_hbm, v_hbm, ranks_hbm, recorded_hbm,
    model_out, resid_out, grad_out,
    w, ranks, recorded, field, total, resid, grad, image, direc,
    sent, held, red_a, red_b, red_c,
    load_sem, small_sem, send_sem, recv_sem,
    red_send, red_recv,
):
    z, x, c = lax.axis_index("z"), lax.axis_index("x"), lax.axis_index("c")
    freq = lax.axis_index("freq")
    place = x * NC + c
    me = z * PLANE + place
    mine = (c * NX + x) * NZ + z

    def across(step):
        half = (step + 1) // 2
        odd = lax.rem(step, 2)
        return lax.rem(NX // 2 + NX + (1 - 2 * odd) * half, NX)

    def offset_of(step):
        half = (step + 1) // 2
        odd = lax.rem(step, 2)
        return lax.rem(NZ // 2 + NZ + (1 - 2 * odd) * half, NZ)

    def at(dz, dx, dc):
        return {"z": lax.rem(z + dz, NZ), "x": lax.rem(x + dx, NX), "c": lax.rem(c + dc, NC)}

    def at_freq(df):
        return {"freq": lax.rem(freq + df, NF)}

    loads = [
        [
            pltpu.make_async_copy(
                hbm.at[:, part % NX, part // NX], w.at[k, part], load_sem.at[k, part]
            )
            for part in range(PLANE)
        ]
        for k, hbm in enumerate((u_hbm, v_hbm))
    ]
    small = [
        pltpu.make_async_copy(recorded_hbm, recorded, small_sem.at[0]),
        pltpu.make_async_copy(ranks_hbm, ranks, small_sem.at[1]),
    ]
    for parts in [small] + loads:
        for load in parts:
            load.start()

    def loaded(k):
        for load in loads[k]:
            load.wait()

    barrier = pltpu.get_barrier_semaphore()

    def greet(step, carry):
        for dx, dc in PLANE_ORDER:
            pl.semaphore_signal(barrier, 1, device_id=at(offset_of(step), dx, dc), device_id_type=MESH)
        return carry

    lax.fori_loop(0, NZ - 1, greet, 0)
    for dx, dc in PLANE_ORDER[:-1]:
        pl.semaphore_signal(barrier, 1, device_id=at(0, dx, dc), device_id_type=MESH)
    for df in range(1, NF):
        pl.semaphore_signal(barrier, 1, device_id=at_freq(df), device_id_type=MESH)

    for load in small:
        load.wait()
    resid[...] = recorded[...].T
    field[...] = resid[...].astype(jnp.bfloat16)
    level = lax.broadcasted_iota(jnp.int32, (RANK, TRACES), 0)

    def partial_squares(value):
        return jnp.sum((value * value).reshape(TRACES // 8, 8, WIDTH // 128, 128), axis=(0, 2)).sum(axis=0, keepdims=True)

    def spread(s, which, count, slot, targets):
        buffer = (red_a, red_b, red_c)[which]
        for target in targets:
            pltpu.make_async_remote_copy(
                src_ref=buffer.at[s, slot],
                dst_ref=buffer.at[s, slot],
                send_sem=red_send.at[s, which],
                recv_sem=red_recv.at[s, which],
                device_id=target,
                device_id_type=MESH,
            ).start()

    def collect(s, which, count):
        buffer = (red_a, red_b, red_c)[which]
        several = buffer.at[s, pl.ds(0, count - 1)]
        pltpu.make_async_copy(several, several, red_recv.at[s, which]).wait()
        pltpu.make_async_copy(several, several, red_send.at[s, which]).wait()
        return jnp.sum(buffer[s], axis=0)

    def sum_first(s, value):
        red_a[s, z] = partial_squares(value)
        spread(s, 0, NZ, z, [at(dz, 0, 0) for dz in ZONE_ORDER if dz])

    def sum_second(s):
        red_b[s, freq] = collect(s, 0, NZ)
        spread(s, 1, NF, freq, [at_freq(df) for df in range(1, NF)])

    def sum_third(s):
        red_c[s, place] = collect(s, 1, NF)
        spread(s, 2, PLANE, place, [at(0, dx, dc) for dx, dc in PLANE_ORDER[:-1]])

    def sum_last(s):
        return jnp.sum(collect(s, 2, PLANE), keepdims=True)

    def apply(app, hooks=(None,) * 4):
        first = app % 2

        def coefficients(part):
            value = lax.dot_general(
                w[first, part].reshape(GROUP, WIDTH),
                field[...],
                (((1,), (1,)), ((), ())),
                preferred_element_type=jnp.float32,
            )
            for t in range(NZ):
                tile = t * PLANE + lax.rem(part, NX) * NC + part // NX
                rank = ranks[me, tile] if first == 0 else ranks[tile, me]
                rows = value[t * RANK : (t + 1) * RANK]
                sent[app, part * NZ + t] = jnp.where(level < rank, rows, 0.0).astype(jnp.bfloat16)

        def send(dz, part):
            slot = part * NZ + lax.rem(z + dz, NZ)
            pltpu.make_async_remote_copy(
                src_ref=sent.at[app, slot],
                dst_ref=held.at[app, mine],
                send_sem=send_sem.at[app],
                recv_sem=recv_sem.at[app, c * NX + x],
                device_id={"z": lax.rem(z + dz, NZ), "x": lax.rem(part, NX), "c": part // NX},
                device_id_type=MESH,
            ).start()

        def part_of(step, sign):
            dx = across(lax.rem(step, NX))
            return (step // NX) * NX + lax.rem(x + sign * dx + NX, NX)

        def send_part(step, carry):
            part = part_of(step, 1)
            coefficients(part)
            if app == 0:
                pl.when(step == 0)(lambda: pl.semaphore_wait(barrier, TILES - 1 + NF - 1))
            for dz in ZONE_ORDER[:-1]:
                send(dz, part)
            pl.when(part != c * NX + x)(lambda: send(0, part))
            return carry

        def hook(k):
            if hooks[k] is not None:
                hooks[k]()

        lax.fori_loop(0, 1, send_part, 0)
        hook(0)
        lax.fori_loop(1, 4, send_part, 0)
        hook(1)
        lax.fori_loop(4, PLANE, send_part, 0)
        own = pltpu.make_async_copy(sent.at[app, mine], held.at[app, mine], recv_sem.at[app, c * NX + x])
        own.start()
        hook(2)

        total[...] = jnp.zeros_like(total)

        def take_part(step, carry):
            part = part_of(step, -1)
            start = pl.multiple_of(part * NZ, NZ)
            group = held.at[app, pl.ds(start, NZ)]
            pltpu.make_async_copy(group, group, recv_sem.at[app, part]).wait()
            value = held[app, pl.ds(start, NZ)].astype(jnp.float32)
            value = value.reshape(GROUP, TRACES).T.astype(jnp.bfloat16)
            total[...] += lax.dot_general(
                value,
                w[1 - first, part].reshape(GROUP, WIDTH),
                (((1,), (0,)), ((), ())),
                preferred_element_type=jnp.float32,
            )
            return carry

        lax.fori_loop(0, PLANE - 1, take_part, 0)
        hook(3)
        lax.fori_loop(PLANE - 1, PLANE, take_part, 0)

    def summing(k, value, late=None):
        return (
            lambda: sum_first(k, value[...]),
            lambda: sum_second(k),
            lambda: sum_third(k),
            late,
        )

    loaded(0)
    apply(0, (None, lambda: loaded(1), None, None))
    grad[...] = total[...]
    field[...] = grad[...].astype(jnp.bfloat16)
    apply(1, summing(0, grad))
    image[...] = total[...]
    field[...] = image[...].astype(jnp.bfloat16)
    apply(2, summing(1, image))
    gamma = sum_last(0)
    delta = sum_last(1)
    alpha = gamma / delta
    direc[...] = grad[...]
    grad[...] = grad[...] - alpha * total[...]
    field[...] = grad[...].astype(jnp.bfloat16)
    def step_resid():
        resid[...] = resid[...] - alpha * image[...]

    apply(3, summing(2, grad, step_resid))
    gamma_new = sum_last(2)
    beta = gamma_new / gamma
    image[...] = total[...] + beta * image[...]
    field[...] = image[...].astype(jnp.bfloat16)

    def finish():
        scale = gamma_new / sum_last(3)
        old = direc[...]
        model_out[...] = (alpha * old + scale * (grad[...] + beta * old)).T
        resid_out[...] = (resid[...] - scale * image[...]).T
        direc[0:1, 0:128] = jnp.broadcast_to(scale, (1, 128))

    apply(4, summing(3, image, finish))
    grad_out[...] = (grad[...] - direc[0:1, 0:1] * total[...]).T

    for app in range(APPS):
        several = sent.at[app, pl.ds(0, TILES - 1)]
        pltpu.make_async_copy(several, several, send_sem.at[app]).wait()


def store(model, resid, grad, model_out, resid_out, grad_out, sem):
    copies = [
        pltpu.make_async_copy(value, out, sem.at[k])
        for k, (value, out) in enumerate(((model, model_out), (resid, resid_out), (grad, grad_out)))
    ]
    for copy in copies:
        copy.start()
    for copy in copies:
        copy.wait()


def local(u_tiles, v_tiles, tile_ranks, recorded):
    rows = TILES * RANK
    field = jax.ShapeDtypeStruct((WIDTH, TRACES), jnp.float32)
    flat = pltpu.VMEM((TRACES, WIDTH), jnp.float32)
    vmem = pl.BlockSpec(memory_space=pltpu.VMEM)
    outs = pl.pallas_call(
        kernel,
        out_shape=(field,) * 3,
        in_specs=[
            pl.BlockSpec(memory_space=pltpu.HBM),
            pl.BlockSpec(memory_space=pltpu.HBM),
            pl.BlockSpec(memory_space=pltpu.HBM),
            pl.BlockSpec(memory_space=pltpu.HBM),
        ],
        out_specs=(vmem,) * 3,
        scratch_shapes=[
            pltpu.VMEM((2, PLANE, NZ, RANK, WIDTH), jnp.bfloat16),
            pltpu.SMEM((TILES, TILES), jnp.int32),
            pltpu.VMEM((WIDTH, TRACES), jnp.float32),
            pltpu.VMEM((TRACES, WIDTH), jnp.bfloat16),
            flat, flat, flat, flat, flat,
            pltpu.VMEM((APPS, TILES, RANK, TRACES), jnp.bfloat16),
            pltpu.VMEM((APPS, TILES, RANK, TRACES), jnp.bfloat16),
            pltpu.VMEM((4, NZ, 1, 128), jnp.float32),
            pltpu.VMEM((4, NF, 1, 128), jnp.float32),
            pltpu.VMEM((4, PLANE, 1, 128), jnp.float32),
            pltpu.SemaphoreType.DMA((2, PLANE)),
            pltpu.SemaphoreType.DMA((2,)),
            pltpu.SemaphoreType.DMA((APPS,)),
            pltpu.SemaphoreType.DMA((APPS, PLANE)),
            pltpu.SemaphoreType.DMA((4, 3)),
            pltpu.SemaphoreType.DMA((4, 3)),
        ],
        compiler_params=pltpu.CompilerParams(
            collective_id=0, has_side_effects=True, vmem_limit_bytes=62 << 20
        ),
        cost_estimate=pl.CostEstimate(
            flops=APPS * 4 * rows * WIDTH * TRACES, bytes_accessed=12 << 20, transcendentals=0
        ),
    )(
        u_tiles.reshape(NZ, NX, NC, RANK, WIDTH),
        v_tiles.reshape(NZ, NX, NC, RANK, WIDTH),
        tile_ranks.reshape(TILES, TILES),
        recorded.reshape(WIDTH, TRACES),
    )
    outs = pl.pallas_call(
        store,
        out_shape=(field,) * 3,
        in_specs=[pl.BlockSpec(memory_space=pltpu.HBM)] * 3,
        out_specs=(pl.BlockSpec(memory_space=pltpu.HBM),) * 3,
        scratch_shapes=[pltpu.SemaphoreType.DMA((3,))],
    )(*outs)
    return tuple(out.reshape(1, WIDTH, TRACES) for out in outs)


def solution(mesh):
    torus = Mesh(mesh.devices.reshape(NZ, NX, NC, NF), ("z", "x", "c", "freq"))
    tile = ("z", "x", "c")
    in_specs = (
        P("freq", tile, None, None, None),
        P("freq", None, tile, None, None),
        P("freq", None, None),
        P("freq", tile, None),
    )
    out_specs = (P("freq", tile, None),) * 3
    return jax.shard_map(local, mesh=torus, in_specs=in_specs, out_specs=out_specs, check_vma=False)
```

```python
import jax
import jax.numpy as jnp
from jax import lax
from jax.experimental import pallas as pl
from jax.experimental.pallas import tpu as pltpu
from jax.sharding import Mesh
from jax.sharding import PartitionSpec as P

MESH = pl.DeviceIdType.MESH
NZ, NX, NC, NF = 8, 4, 2, 4
RANK, WIDTH, TRACES = 40, 1024, 128
PLANE = NX * NC
GROUP = NZ * RANK
TILES = NZ * PLANE
APPS = 5
PLANE_ORDER = ((2, 1), (2, 0), (1, 1), (3, 1), (1, 0), (3, 0), (0, 1), (0, 0))
ZONE_ORDER = (4, 3, 5, 2, 6, 1, 7, 0)


def kernel(
    u_hbm, v_hbm, ranks_hbm, recorded_hbm,
    model_out, resid_out, grad_out,
    w, ranks, recorded, field, total, resid, grad, image, direc,
    sent, held, red_a, red_b, red_c,
    load_sem, small_sem, send_sem, recv_sem,
    red_send, red_recv,
):
    z, x, c = lax.axis_index("z"), lax.axis_index("x"), lax.axis_index("c")
    freq = lax.axis_index("freq")
    place = x * NC + c
    me = z * PLANE + place
    mine = (c * NX + x) * NZ + z

    def across(step):
        half = (step + 1) // 2
        odd = lax.rem(step, 2)
        return lax.rem(NX // 2 + NX + (1 - 2 * odd) * half, NX)

    def offset_of(step):
        half = (step + 1) // 2
        odd = lax.rem(step, 2)
        return lax.rem(NZ // 2 + NZ + (1 - 2 * odd) * half, NZ)

    def at(dz, dx, dc):
        return {"z": lax.rem(z + dz, NZ), "x": lax.rem(x + dx, NX), "c": lax.rem(c + dc, NC)}

    def at_freq(df):
        return {"freq": lax.rem(freq + df, NF)}

    loads = [
        [
            pltpu.make_async_copy(
                hbm.at[:, part % NX, part // NX], w.at[k, part], load_sem.at[k, part]
            )
            for part in range(PLANE)
        ]
        for k, hbm in enumerate((u_hbm, v_hbm))
    ]
    small = [
        pltpu.make_async_copy(recorded_hbm, recorded, small_sem.at[0]),
        pltpu.make_async_copy(ranks_hbm, ranks, small_sem.at[1]),
    ]
    for parts in [small] + loads:
        for load in parts:
            load.start()

    def loaded(k):
        for load in loads[k]:
            load.wait()

    barrier = pltpu.get_barrier_semaphore()

    def greet(step, carry):
        for dx, dc in PLANE_ORDER:
            pl.semaphore_signal(barrier, 1, device_id=at(offset_of(step), dx, dc), device_id_type=MESH)
        return carry

    lax.fori_loop(0, NZ - 1, greet, 0)
    for dx, dc in PLANE_ORDER[:-1]:
        pl.semaphore_signal(barrier, 1, device_id=at(0, dx, dc), device_id_type=MESH)
    for df in range(1, NF):
        pl.semaphore_signal(barrier, 1, device_id=at_freq(df), device_id_type=MESH)

    for load in small:
        load.wait()
    resid[...] = recorded[...].T
    field[...] = resid[...].astype(jnp.bfloat16)
    level = lax.broadcasted_iota(jnp.int32, (RANK, TRACES), 0)

    def partial_squares(value):
        return jnp.sum((value * value).reshape(TRACES // 8, 8, WIDTH // 128, 128), axis=(0, 2)).sum(axis=0, keepdims=True)

    def spread(s, which, count, slot, targets):
        buffer = (red_a, red_b, red_c)[which]
        for target in targets:
            pltpu.make_async_remote_copy(
                src_ref=buffer.at[s, slot],
                dst_ref=buffer.at[s, slot],
                send_sem=red_send.at[s, which],
                recv_sem=red_recv.at[s, which],
                device_id=target,
                device_id_type=MESH,
            ).start()

    def collect(s, which, count):
        buffer = (red_a, red_b, red_c)[which]
        several = buffer.at[s, pl.ds(0, count - 1)]
        pltpu.make_async_copy(several, several, red_recv.at[s, which]).wait()
        pltpu.make_async_copy(several, several, red_send.at[s, which]).wait()
        return jnp.sum(buffer[s], axis=0)

    def sum_first(s, value):
        red_a[s, z] = partial_squares(value)
        spread(s, 0, NZ, z, [at(dz, 0, 0) for dz in ZONE_ORDER if dz])

    def sum_second(s):
        red_b[s, freq] = collect(s, 0, NZ)
        spread(s, 1, NF, freq, [at_freq(df) for df in range(1, NF)])

    def sum_third(s):
        red_c[s, place] = collect(s, 1, NF)
        spread(s, 2, PLANE, place, [at(0, dx, dc) for dx, dc in PLANE_ORDER[:-1]])

    def sum_last(s):
        return jnp.sum(collect(s, 2, PLANE), keepdims=True)

    def apply(app, hooks=(None,) * 4):
        first = app % 2

        def coefficients(part):
            value = lax.dot_general(
                w[first, part].reshape(GROUP, WIDTH),
                field[...],
                (((1,), (1,)), ((), ())),
                preferred_element_type=jnp.float32,
            )
            for t in range(NZ):
                tile = t * PLANE + lax.rem(part, NX) * NC + part // NX
                rank = ranks[me, tile] if first == 0 else ranks[tile, me]
                rows = value[t * RANK : (t + 1) * RANK]
                sent[app, part * NZ + t] = jnp.where(level < rank, rows, 0.0).astype(jnp.bfloat16)

        def send(dz, part):
            slot = part * NZ + lax.rem(z + dz, NZ)
            pltpu.make_async_remote_copy(
                src_ref=sent.at[app, slot],
                dst_ref=held.at[app, mine],
                send_sem=send_sem.at[app],
                recv_sem=recv_sem.at[app, c * NX + x],
                device_id={"z": lax.rem(z + dz, NZ), "x": lax.rem(part, NX), "c": part // NX},
                device_id_type=MESH,
            ).start()

        def part_of(step, sign):
            dx = across(lax.rem(step, NX))
            return (step // NX) * NX + lax.rem(x + sign * dx + NX, NX)

        def send_part(step, carry):
            part = part_of(step, 1)
            coefficients(part)
            if app == 0:
                pl.when(step == 0)(lambda: pl.semaphore_wait(barrier, TILES - 1 + NF - 1))
            for dz in ZONE_ORDER[:-1]:
                send(dz, part)
            pl.when(part != c * NX + x)(lambda: send(0, part))
            return carry

        def hook(k):
            if hooks[k] is not None:
                hooks[k]()

        hook(0)
        lax.fori_loop(0, 6, send_part, 0)
        hook(1)
        lax.fori_loop(6, PLANE, send_part, 0)
        own = pltpu.make_async_copy(sent.at[app, mine], held.at[app, mine], recv_sem.at[app, c * NX + x])
        own.start()

        total[...] = jnp.zeros_like(total)

        def take_part(step, carry):
            part = part_of(step, -1)
            start = pl.multiple_of(part * NZ, NZ)
            group = held.at[app, pl.ds(start, NZ)]
            pltpu.make_async_copy(group, group, recv_sem.at[app, part]).wait()
            value = held[app, pl.ds(start, NZ)].astype(jnp.float32)
            value = value.reshape(GROUP, TRACES).T.astype(jnp.bfloat16)
            total[...] += lax.dot_general(
                value,
                w[1 - first, part].reshape(GROUP, WIDTH),
                (((1,), (0,)), ((), ())),
                preferred_element_type=jnp.float32,
            )
            return carry

        lax.fori_loop(0, 1, take_part, 0)
        hook(2)
        lax.fori_loop(1, PLANE - 1, take_part, 0)
        hook(3)
        lax.fori_loop(PLANE - 1, PLANE, take_part, 0)

    def summing(k, value, late=None):
        return (
            lambda: sum_first(k, value[...]),
            lambda: sum_second(k),
            lambda: sum_third(k),
            late,
        )

    loaded(0)
    apply(0, (None, lambda: loaded(1), None, None))
    grad[...] = total[...]
    field[...] = grad[...].astype(jnp.bfloat16)
    apply(1, summing(0, grad))
    image[...] = total[...]
    field[...] = image[...].astype(jnp.bfloat16)
    apply(2, summing(1, image))
    gamma = sum_last(0)
    delta = sum_last(1)
    alpha = gamma / delta
    direc[...] = grad[...]
    grad[...] = grad[...] - alpha * total[...]
    field[...] = grad[...].astype(jnp.bfloat16)
    def step_resid():
        resid[...] = resid[...] - alpha * image[...]

    apply(3, summing(2, grad, step_resid))
    gamma_new = sum_last(2)
    beta = gamma_new / gamma
    image[...] = total[...] + beta * image[...]
    field[...] = image[...].astype(jnp.bfloat16)

    def finish():
        scale = gamma_new / sum_last(3)
        old = direc[...]
        model_out[...] = (alpha * old + scale * (grad[...] + beta * old)).T
        resid_out[...] = (resid[...] - scale * image[...]).T
        direc[0:1, 0:128] = jnp.broadcast_to(scale, (1, 128))

    apply(4, summing(3, image, finish))
    grad_out[...] = (grad[...] - direc[0:1, 0:1] * total[...]).T

    for app in range(APPS):
        several = sent.at[app, pl.ds(0, TILES - 1)]
        pltpu.make_async_copy(several, several, send_sem.at[app]).wait()


def store(model, resid, grad, model_out, resid_out, grad_out, sem):
    copies = [
        pltpu.make_async_copy(value, out, sem.at[k])
        for k, (value, out) in enumerate(((model, model_out), (resid, resid_out), (grad, grad_out)))
    ]
    for copy in copies:
        copy.start()
    for copy in copies:
        copy.wait()


def local(u_tiles, v_tiles, tile_ranks, recorded):
    rows = TILES * RANK
    field = jax.ShapeDtypeStruct((WIDTH, TRACES), jnp.float32)
    flat = pltpu.VMEM((TRACES, WIDTH), jnp.float32)
    vmem = pl.BlockSpec(memory_space=pltpu.VMEM)
    outs = pl.pallas_call(
        kernel,
        out_shape=(field,) * 3,
        in_specs=[
            pl.BlockSpec(memory_space=pltpu.HBM),
            pl.BlockSpec(memory_space=pltpu.HBM),
            pl.BlockSpec(memory_space=pltpu.HBM),
            pl.BlockSpec(memory_space=pltpu.HBM),
        ],
        out_specs=(vmem,) * 3,
        scratch_shapes=[
            pltpu.VMEM((2, PLANE, NZ, RANK, WIDTH), jnp.bfloat16),
            pltpu.SMEM((TILES, TILES), jnp.int32),
            pltpu.VMEM((WIDTH, TRACES), jnp.float32),
            pltpu.VMEM((TRACES, WIDTH), jnp.bfloat16),
            flat, flat, flat, flat, flat,
            pltpu.VMEM((APPS, TILES, RANK, TRACES), jnp.bfloat16),
            pltpu.VMEM((APPS, TILES, RANK, TRACES), jnp.bfloat16),
            pltpu.VMEM((4, NZ, 1, 128), jnp.float32),
            pltpu.VMEM((4, NF, 1, 128), jnp.float32),
            pltpu.VMEM((4, PLANE, 1, 128), jnp.float32),
            pltpu.SemaphoreType.DMA((2, PLANE)),
            pltpu.SemaphoreType.DMA((2,)),
            pltpu.SemaphoreType.DMA((APPS,)),
            pltpu.SemaphoreType.DMA((APPS, PLANE)),
            pltpu.SemaphoreType.DMA((4, 3)),
            pltpu.SemaphoreType.DMA((4, 3)),
        ],
        compiler_params=pltpu.CompilerParams(
            collective_id=0, has_side_effects=True, vmem_limit_bytes=62 << 20
        ),
        cost_estimate=pl.CostEstimate(
            flops=APPS * 4 * rows * WIDTH * TRACES, bytes_accessed=12 << 20, transcendentals=0
        ),
    )(
        u_tiles.reshape(NZ, NX, NC, RANK, WIDTH),
        v_tiles.reshape(NZ, NX, NC, RANK, WIDTH),
        tile_ranks.reshape(TILES, TILES),
        recorded.reshape(WIDTH, TRACES),
    )
    outs = pl.pallas_call(
        store,
        out_shape=(field,) * 3,
        in_specs=[vmem] * 3,
        out_specs=(pl.BlockSpec(memory_space=pltpu.HBM),) * 3,
        scratch_shapes=[pltpu.SemaphoreType.DMA((3,))],
    )(*outs)
    return tuple(out.reshape(1, WIDTH, TRACES) for out in outs)


def solution(mesh):
    torus = Mesh(mesh.devices.reshape(NZ, NX, NC, NF), ("z", "x", "c", "freq"))
    tile = ("z", "x", "c")
    in_specs = (
        P("freq", tile, None, None, None),
        P("freq", None, tile, None, None),
        P("freq", None, None),
        P("freq", tile, None),
    )
    out_specs = (P("freq", tile, None),) * 3
    return jax.shard_map(local, mesh=torus, in_specs=in_specs, out_specs=out_specs, check_vma=False)
```

```python
import jax
import jax.numpy as jnp
from jax import lax
from jax.experimental import pallas as pl
from jax.experimental.pallas import tpu as pltpu
from jax.sharding import Mesh
from jax.sharding import PartitionSpec as P

MESH = pl.DeviceIdType.MESH
NZ, NX, NC, NF = 8, 4, 2, 4
RANK, WIDTH, TRACES = 40, 1024, 128
PLANE = NX * NC
GROUP = NZ * RANK
TILES = NZ * PLANE
APPS = 5
CHUNKS = 4
PLANE_ORDER = ((2, 1), (2, 0), (1, 1), (3, 1), (1, 0), (3, 0), (0, 1), (0, 0))
ZONE_ORDER = (4, 3, 5, 2, 6, 1, 7, 0)


def kernel(
    u_hbm, v_hbm, ranks_hbm, recorded_hbm,
    model_hbm, resid_hbm, grad_hbm,
    w, ranks, recorded, field, total, resid, grad, image, direc,
    sent, held, red_a, red_b, red_c,
    load_sem, small_sem, send_sem, recv_sem,
    red_send, red_recv,
    model_out, resid_out, grad_out, out_sem,
):
    z, x, c = lax.axis_index("z"), lax.axis_index("x"), lax.axis_index("c")
    freq = lax.axis_index("freq")
    place = x * NC + c
    me = z * PLANE + place
    mine = (c * NX + x) * NZ + z

    def across(step):
        half = (step + 1) // 2
        odd = lax.rem(step, 2)
        return lax.rem(NX // 2 + NX + (1 - 2 * odd) * half, NX)

    def offset_of(step):
        half = (step + 1) // 2
        odd = lax.rem(step, 2)
        return lax.rem(NZ // 2 + NZ + (1 - 2 * odd) * half, NZ)

    def at(dz, dx, dc):
        return {"z": lax.rem(z + dz, NZ), "x": lax.rem(x + dx, NX), "c": lax.rem(c + dc, NC)}

    def at_freq(df):
        return {"freq": lax.rem(freq + df, NF)}

    barrier = pltpu.get_barrier_semaphore()

    def greet(step, carry):
        for dx, dc in PLANE_ORDER:
            pl.semaphore_signal(barrier, 1, device_id=at(offset_of(step), dx, dc), device_id_type=MESH)
        return carry

    lax.fori_loop(0, NZ - 1, greet, 0)
    for dx, dc in PLANE_ORDER[:-1]:
        pl.semaphore_signal(barrier, 1, device_id=at(0, dx, dc), device_id_type=MESH)
    for df in range(1, NF):
        pl.semaphore_signal(barrier, 1, device_id=at_freq(df), device_id_type=MESH)

    loads = [
        [
            pltpu.make_async_copy(
                hbm.at[:, part % NX, part // NX], w.at[k, part], load_sem.at[k, part]
            )
            for part in range(PLANE)
        ]
        for k, hbm in enumerate((u_hbm, v_hbm))
    ]
    small = [
        pltpu.make_async_copy(recorded_hbm, recorded, small_sem.at[0]),
        pltpu.make_async_copy(ranks_hbm, ranks, small_sem.at[1]),
    ]
    for parts in [small] + loads:
        for load in parts:
            load.start()

    def loaded(k):
        for load in loads[k]:
            load.wait()

    for load in small:
        load.wait()
    resid[...] = recorded[...].T
    field[...] = resid[...].astype(jnp.bfloat16)
    level = lax.broadcasted_iota(jnp.int32, (RANK, TRACES), 0)

    def partial_squares(value):
        return jnp.sum((value * value).reshape(TRACES // 8, 8, WIDTH // 128, 128), axis=(0, 2)).sum(axis=0, keepdims=True)

    def spread(s, which, count, slot, targets):
        buffer = (red_a, red_b, red_c)[which]
        for target in targets:
            pltpu.make_async_remote_copy(
                src_ref=buffer.at[s, slot],
                dst_ref=buffer.at[s, slot],
                send_sem=red_send.at[s, which],
                recv_sem=red_recv.at[s, which],
                device_id=target,
                device_id_type=MESH,
            ).start()

    def collect(s, which, count):
        buffer = (red_a, red_b, red_c)[which]
        several = buffer.at[s, pl.ds(0, count - 1)]
        pltpu.make_async_copy(several, several, red_recv.at[s, which]).wait()
        pltpu.make_async_copy(several, several, red_send.at[s, which]).wait()
        return jnp.sum(buffer[s], axis=0)

    def sum_first(s, value):
        red_a[s, z] = partial_squares(value)
        spread(s, 0, NZ, z, [at(dz, 0, 0) for dz in ZONE_ORDER if dz])

    def sum_second(s):
        red_b[s, freq] = collect(s, 0, NZ)
        spread(s, 1, NF, freq, [at_freq(df) for df in range(1, NF)])

    def sum_third(s):
        red_c[s, place] = collect(s, 1, NF)
        spread(s, 2, PLANE, place, [at(0, dx, dc) for dx, dc in PLANE_ORDER[:-1]])

    def sum_last(s):
        return jnp.sum(collect(s, 2, PLANE), keepdims=True)

    def apply(app, hooks=(None,) * 4):
        first = app % 2

        def coefficients(part):
            value = lax.dot_general(
                w[first, part].reshape(GROUP, WIDTH),
                field[...],
                (((1,), (1,)), ((), ())),
                preferred_element_type=jnp.float32,
            )
            for t in range(NZ):
                tile = t * PLANE + lax.rem(part, NX) * NC + part // NX
                rank = ranks[me, tile] if first == 0 else ranks[tile, me]
                rows = value[t * RANK : (t + 1) * RANK]
                sent[app, part * NZ + t] = jnp.where(level < rank, rows, 0.0).astype(jnp.bfloat16)

        def send(dz, part):
            slot = part * NZ + lax.rem(z + dz, NZ)
            pltpu.make_async_remote_copy(
                src_ref=sent.at[app, slot],
                dst_ref=held.at[app, mine],
                send_sem=send_sem.at[app],
                recv_sem=recv_sem.at[app, c * NX + x],
                device_id={"z": lax.rem(z + dz, NZ), "x": lax.rem(part, NX), "c": part // NX},
                device_id_type=MESH,
            ).start()

        def part_of(step, sign):
            dx = across(lax.rem(step, NX))
            return (step // NX) * NX + lax.rem(x + sign * dx + NX, NX)

        def send_part(step, carry):
            part = part_of(step, 1)
            coefficients(part)
            if app == 0:
                pl.when(step == 0)(lambda: pl.semaphore_wait(barrier, TILES - 1 + NF - 1))
            for dz in ZONE_ORDER[:-1]:
                send(dz, part)
            pl.when(part != c * NX + x)(lambda: send(0, part))
            return carry

        def hook(k):
            if hooks[k] is not None:
                hooks[k]()

        hook(0)
        lax.fori_loop(0, 6, send_part, 0)
        hook(1)
        lax.fori_loop(6, PLANE, send_part, 0)
        own = pltpu.make_async_copy(sent.at[app, mine], held.at[app, mine], recv_sem.at[app, c * NX + x])
        own.start()

        total[...] = jnp.zeros_like(total)

        def take_part(step, carry):
            part = part_of(step, -1)
            start = pl.multiple_of(part * NZ, NZ)
            group = held.at[app, pl.ds(start, NZ)]
            pltpu.make_async_copy(group, group, recv_sem.at[app, part]).wait()
            value = held[app, pl.ds(start, NZ)].astype(jnp.float32)
            value = value.reshape(GROUP, TRACES).T.astype(jnp.bfloat16)
            total[...] += lax.dot_general(
                value,
                w[1 - first, part].reshape(GROUP, WIDTH),
                (((1,), (0,)), ((), ())),
                preferred_element_type=jnp.float32,
            )
            return carry

        lax.fori_loop(0, 1, take_part, 0)
        hook(2)
        lax.fori_loop(1, PLANE - 1, take_part, 0)
        hook(3)
        lax.fori_loop(PLANE - 1, PLANE, take_part, 0)

    def summing(k, value, late=None):
        return (
            lambda: sum_first(k, value[...]),
            lambda: sum_second(k),
            lambda: sum_third(k),
            late,
        )

    loaded(0)
    apply(0, (None, lambda: loaded(1), None, None))
    grad[...] = total[...]
    field[...] = grad[...].astype(jnp.bfloat16)
    apply(1, summing(0, grad))
    image[...] = total[...]
    field[...] = image[...].astype(jnp.bfloat16)
    apply(2, summing(1, image))
    gamma = sum_last(0)
    delta = sum_last(1)
    alpha = gamma / delta
    direc[...] = grad[...]
    grad[...] = grad[...] - alpha * total[...]
    field[...] = grad[...].astype(jnp.bfloat16)
    def step_resid():
        resid[...] = resid[...] - alpha * image[...]

    apply(3, summing(2, grad, step_resid))
    gamma_new = sum_last(2)
    beta = gamma_new / gamma
    image[...] = total[...] + beta * image[...]
    field[...] = image[...].astype(jnp.bfloat16)

    early = [
        pltpu.make_async_copy(value, hbm, out_sem.at[k])
        for k, (value, hbm) in enumerate(((model_out, model_hbm), (resid_out, resid_hbm)))
    ]

    def finish():
        scale = gamma_new / sum_last(3)
        old = direc[...]
        model_out[...] = (alpha * old + scale * (grad[...] + beta * old)).T
        resid_out[...] = (resid[...] - scale * image[...]).T
        direc[0:1, 0:128] = jnp.broadcast_to(scale, (1, 128))
        for copy in early:
            copy.start()

    apply(4, summing(3, image, finish))
    late = []
    for k in range(CHUNKS):
        part = pl.ds(k * WIDTH // CHUNKS, WIDTH // CHUNKS)
        grad_out[part] = (grad[:, part] - direc[0:1, 0:1] * total[:, part]).T
        late.append(pltpu.make_async_copy(grad_out.at[part], grad_hbm.at[part], out_sem.at[2 + k]))
        late[k].start()

    for app in range(APPS):
        several = sent.at[app, pl.ds(0, TILES - 1)]
        pltpu.make_async_copy(several, several, send_sem.at[app]).wait()
    for copy in early + late:
        copy.wait()


def store(model, resid, grad, model_out, resid_out, grad_out, held, in_sem, out_sem):
    pairs = ((model, model_out), (resid, resid_out), (grad, grad_out))
    size = WIDTH // CHUNKS
    parts = [(k, j, pl.ds(j * size, size)) for k in range(3) for j in range(CHUNKS)]
    takes = [pltpu.make_async_copy(pairs[k][0].at[p], held.at[k, p], in_sem.at[k, j]) for k, j, p in parts]
    gives = [pltpu.make_async_copy(held.at[k, p], pairs[k][1].at[p], out_sem.at[k, j]) for k, j, p in parts]
    for take in takes:
        take.start()
    for take, give in zip(takes, gives):
        take.wait()
        give.start()
    for give in gives:
        give.wait()


def local(u_tiles, v_tiles, tile_ranks, recorded):
    rows = TILES * RANK
    field = jax.ShapeDtypeStruct((WIDTH, TRACES), jnp.float32)
    flat = pltpu.VMEM((TRACES, WIDTH), jnp.float32)
    hbm = pl.BlockSpec(memory_space=pltpu.HBM)
    outs = pl.pallas_call(
        kernel,
        out_shape=(field,) * 3,
        in_specs=[
            hbm,
            hbm,
            hbm,
            hbm,
        ],
        out_specs=(hbm,) * 3,
        scratch_shapes=[
            pltpu.VMEM((2, PLANE, NZ, RANK, WIDTH), jnp.bfloat16),
            pltpu.SMEM((TILES, TILES), jnp.int32),
            pltpu.VMEM((WIDTH, TRACES), jnp.float32),
            pltpu.VMEM((TRACES, WIDTH), jnp.bfloat16),
            flat, flat, flat, flat, flat,
            pltpu.VMEM((APPS, TILES, RANK, TRACES), jnp.bfloat16),
            pltpu.VMEM((APPS, TILES, RANK, TRACES), jnp.bfloat16),
            pltpu.VMEM((4, NZ, 1, 128), jnp.float32),
            pltpu.VMEM((4, NF, 1, 128), jnp.float32),
            pltpu.VMEM((4, PLANE, 1, 128), jnp.float32),
            pltpu.SemaphoreType.DMA((2, PLANE)),
            pltpu.SemaphoreType.DMA((2,)),
            pltpu.SemaphoreType.DMA((APPS,)),
            pltpu.SemaphoreType.DMA((APPS, PLANE)),
            pltpu.SemaphoreType.DMA((4, 3)),
            pltpu.SemaphoreType.DMA((4, 3)),
            pltpu.VMEM((WIDTH, TRACES), jnp.float32),
            pltpu.VMEM((WIDTH, TRACES), jnp.float32),
            pltpu.VMEM((WIDTH, TRACES), jnp.float32),
            pltpu.SemaphoreType.DMA((2 + CHUNKS,)),
        ],
        compiler_params=pltpu.CompilerParams(
            collective_id=0, has_side_effects=True, vmem_limit_bytes=62 << 20
        ),
        cost_estimate=pl.CostEstimate(
            flops=APPS * 4 * rows * WIDTH * TRACES, bytes_accessed=12 << 20, transcendentals=0
        ),
    )(
        u_tiles.reshape(NZ, NX, NC, RANK, WIDTH),
        v_tiles.reshape(NZ, NX, NC, RANK, WIDTH),
        tile_ranks.reshape(TILES, TILES),
        recorded.reshape(WIDTH, TRACES),
    )
    outs = pl.pallas_call(
        store,
        out_shape=(field,) * 3,
        in_specs=[hbm] * 3,
        out_specs=(hbm,) * 3,
        scratch_shapes=[
            pltpu.VMEM((3, WIDTH, TRACES), jnp.float32),
            pltpu.SemaphoreType.DMA((3, CHUNKS)),
            pltpu.SemaphoreType.DMA((3, CHUNKS)),
        ],
    )(*outs)
    return tuple(out.reshape(1, WIDTH, TRACES) for out in outs)


def solution(mesh):
    torus = Mesh(mesh.devices.reshape(NZ, NX, NC, NF), ("z", "x", "c", "freq"))
    tile = ("z", "x", "c")
    in_specs = (
        P("freq", tile, None, None, None),
        P("freq", None, tile, None, None),
        P("freq", None, None),
        P("freq", tile, None),
    )
    out_specs = (P("freq", tile, None),) * 3
    return jax.shard_map(local, mesh=torus, in_specs=in_specs, out_specs=out_specs, check_vma=False)
```

```python
import jax
import jax.numpy as jnp
from jax import lax
from jax.experimental import pallas as pl
from jax.experimental.pallas import tpu as pltpu
from jax.sharding import Mesh
from jax.sharding import PartitionSpec as P

MESH = pl.DeviceIdType.MESH
NZ, NX, NC, NF = 8, 4, 2, 4
RANK, WIDTH, TRACES = 40, 1024, 128
PLANE = NX * NC
GROUP = NZ * RANK
TILES = NZ * PLANE
APPS = 5
CHUNKS = 4
PLANE_ORDER = ((2, 1), (2, 0), (1, 1), (3, 1), (1, 0), (3, 0), (0, 1), (0, 0))
ZONE_ORDER = (4, 3, 5, 2, 6, 1, 7, 0)


def kernel(
    u_hbm, v_hbm, ranks_hbm, recorded_hbm,
    model_hbm, resid_hbm, grad_hbm,
    w, ranks, recorded, field, total, resid, grad, image, direc,
    sent, held, red_a, red_b, red_c,
    load_sem, small_sem, send_sem, recv_sem,
    red_send, red_recv,
    model_out, resid_out, grad_out, out_sem, ready,
):
    z, x, c = lax.axis_index("z"), lax.axis_index("x"), lax.axis_index("c")
    freq = lax.axis_index("freq")
    place = x * NC + c
    me = z * PLANE + place
    mine = (c * NX + x) * NZ + z

    def across(step):
        half = (step + 1) // 2
        odd = lax.rem(step, 2)
        return lax.rem(NX // 2 + NX + (1 - 2 * odd) * half, NX)

    def offset_of(step):
        half = (step + 1) // 2
        odd = lax.rem(step, 2)
        return lax.rem(NZ // 2 + NZ + (1 - 2 * odd) * half, NZ)

    def at(dz, dx, dc):
        return {"z": lax.rem(z + dz, NZ), "x": lax.rem(x + dx, NX), "c": lax.rem(c + dc, NC)}

    def at_freq(df):
        return {"freq": lax.rem(freq + df, NF)}

    barrier = pltpu.get_barrier_semaphore()

    def greet(step, carry):
        for dx in (2, 1, 3, 0):
            pl.semaphore_signal(barrier, 1, device_id=at(offset_of(step), dx, 0), device_id_type=MESH)
        return carry

    lax.fori_loop(0, NZ - 1, greet, 0)
    for dx in (2, 1, 3):
        pl.semaphore_signal(barrier, 1, device_id=at(0, dx, 0), device_id_type=MESH)
    for df in range(1, NF):
        pl.semaphore_signal(barrier, 1, device_id=at_freq(df), device_id_type=MESH)

    def tell(semaphore):
        pl.semaphore_signal(semaphore, 1, device_id={"c": 1 - c}, device_id_type=MESH)

    pl.when(c == 1)(lambda: tell(barrier))

    def enter():
        pl.semaphore_wait(barrier, NZ * NX - 1 + NF - 1 + 1 - c)

    def ask():
        tell(ready)
        pl.semaphore_wait(ready, 1)

    def answer():
        pl.semaphore_wait(ready, 1)
        tell(ready)

    loads = [
        [
            pltpu.make_async_copy(
                hbm.at[:, part % NX, part // NX], w.at[k, part], load_sem.at[k, part]
            )
            for part in range(PLANE)
        ]
        for k, hbm in enumerate((u_hbm, v_hbm))
    ]
    small = [
        pltpu.make_async_copy(recorded_hbm, recorded, small_sem.at[0]),
        pltpu.make_async_copy(ranks_hbm, ranks, small_sem.at[1]),
    ]
    for parts in [small] + loads:
        for load in parts:
            load.start()

    def loaded(k):
        for load in loads[k]:
            load.wait()

    for load in small:
        load.wait()
    resid[...] = recorded[...].T
    field[...] = resid[...].astype(jnp.bfloat16)
    level = lax.broadcasted_iota(jnp.int32, (RANK, TRACES), 0)

    def partial_squares(value):
        return jnp.sum((value * value).reshape(TRACES // 8, 8, WIDTH // 128, 128), axis=(0, 2)).sum(axis=0, keepdims=True)

    def spread(s, which, count, slot, targets):
        buffer = (red_a, red_b, red_c)[which]
        for target in targets:
            pltpu.make_async_remote_copy(
                src_ref=buffer.at[s, slot],
                dst_ref=buffer.at[s, slot],
                send_sem=red_send.at[s, which],
                recv_sem=red_recv.at[s, which],
                device_id=target,
                device_id_type=MESH,
            ).start()

    def collect(s, which, count):
        buffer = (red_a, red_b, red_c)[which]
        several = buffer.at[s, pl.ds(0, count - 1)]
        pltpu.make_async_copy(several, several, red_recv.at[s, which]).wait()
        pltpu.make_async_copy(several, several, red_send.at[s, which]).wait()
        return jnp.sum(buffer[s], axis=0)

    def sum_first(s, value):
        red_a[s, z] = partial_squares(value)
        spread(s, 0, NZ, z, [at(dz, 0, 0) for dz in ZONE_ORDER if dz])

    def sum_second(s):
        red_b[s, freq] = collect(s, 0, NZ)
        spread(s, 1, NF, freq, [at_freq(df) for df in range(1, NF)])

    def sum_third(s):
        red_c[s, place] = collect(s, 1, NF)
        spread(s, 2, PLANE, place, [at(0, dx, dc) for dx, dc in PLANE_ORDER[:-1]])

    def sum_last(s):
        return jnp.sum(collect(s, 2, PLANE), keepdims=True)

    def apply(app, hooks=(None,) * 4):
        first = app % 2

        def coefficients(part):
            value = lax.dot_general(
                w[first, part].reshape(GROUP, WIDTH),
                field[...],
                (((1,), (1,)), ((), ())),
                preferred_element_type=jnp.float32,
            )
            for t in range(NZ):
                tile = t * PLANE + lax.rem(part, NX) * NC + part // NX
                rank = ranks[me, tile] if first == 0 else ranks[tile, me]
                rows = value[t * RANK : (t + 1) * RANK]
                sent[app, part * NZ + t] = jnp.where(level < rank, rows, 0.0).astype(jnp.bfloat16)

        def send(dz, part):
            slot = part * NZ + lax.rem(z + dz, NZ)
            pltpu.make_async_remote_copy(
                src_ref=sent.at[app, slot],
                dst_ref=held.at[app, mine],
                send_sem=send_sem.at[app],
                recv_sem=recv_sem.at[app, c * NX + x],
                device_id={"z": lax.rem(z + dz, NZ), "x": lax.rem(part, NX), "c": part // NX},
                device_id_type=MESH,
            ).start()

        def part_of(step, sign):
            dx = across(lax.rem(step, NX))
            return (1 - step // NX) * NX + lax.rem(x + sign * dx + NX, NX)

        def send_part(step, carry):
            part = part_of(step, 1)
            coefficients(part)
            if app == 0:
                pl.when(step == 0)(enter)
                pl.when((step == 0) & (c == 0))(ask)
                pl.when((step == NX) & (c == 1))(answer)
            for dz in ZONE_ORDER[:-1]:
                send(dz, part)
            pl.when(part != c * NX + x)(lambda: send(0, part))
            return carry

        def hook(k):
            if hooks[k] is not None:
                hooks[k]()

        hook(0)
        lax.fori_loop(0, 6, send_part, 0)
        hook(1)
        lax.fori_loop(6, PLANE, send_part, 0)
        own = pltpu.make_async_copy(sent.at[app, mine], held.at[app, mine], recv_sem.at[app, c * NX + x])
        own.start()

        total[...] = jnp.zeros_like(total)

        def take_part(step, carry):
            part = part_of(step, -1)
            start = pl.multiple_of(part * NZ, NZ)
            group = held.at[app, pl.ds(start, NZ)]
            pltpu.make_async_copy(group, group, recv_sem.at[app, part]).wait()
            value = held[app, pl.ds(start, NZ)].astype(jnp.float32)
            value = value.reshape(GROUP, TRACES).T.astype(jnp.bfloat16)
            total[...] += lax.dot_general(
                value,
                w[1 - first, part].reshape(GROUP, WIDTH),
                (((1,), (0,)), ((), ())),
                preferred_element_type=jnp.float32,
            )
            return carry

        lax.fori_loop(0, 1, take_part, 0)
        hook(2)
        lax.fori_loop(1, PLANE - 1, take_part, 0)
        hook(3)
        lax.fori_loop(PLANE - 1, PLANE, take_part, 0)

    def summing(k, value, late=None):
        return (
            lambda: sum_first(k, value[...]),
            lambda: sum_second(k),
            lambda: sum_third(k),
            late,
        )

    loaded(0)
    apply(0, (None, lambda: loaded(1), None, None))
    grad[...] = total[...]
    field[...] = grad[...].astype(jnp.bfloat16)
    apply(1, summing(0, grad))
    image[...] = total[...]
    field[...] = image[...].astype(jnp.bfloat16)
    apply(2, summing(1, image))
    gamma = sum_last(0)
    delta = sum_last(1)
    alpha = gamma / delta
    direc[...] = grad[...]
    grad[...] = grad[...] - alpha * total[...]
    field[...] = grad[...].astype(jnp.bfloat16)
    def step_resid():
        resid[...] = resid[...] - alpha * image[...]

    apply(3, summing(2, grad, step_resid))
    gamma_new = sum_last(2)
    beta = gamma_new / gamma
    image[...] = total[...] + beta * image[...]
    field[...] = image[...].astype(jnp.bfloat16)

    early = [
        pltpu.make_async_copy(value, hbm, out_sem.at[k])
        for k, (value, hbm) in enumerate(((model_out, model_hbm), (resid_out, resid_hbm)))
    ]

    def finish():
        scale = gamma_new / sum_last(3)
        old = direc[...]
        model_out[...] = (alpha * old + scale * (grad[...] + beta * old)).T
        resid_out[...] = (resid[...] - scale * image[...]).T
        direc[0:1, 0:128] = jnp.broadcast_to(scale, (1, 128))
        for copy in early:
            copy.start()

    apply(4, summing(3, image, finish))
    late = []
    for k in range(CHUNKS):
        part = pl.ds(k * WIDTH // CHUNKS, WIDTH // CHUNKS)
        grad_out[part] = (grad[:, part] - direc[0:1, 0:1] * total[:, part]).T
        late.append(pltpu.make_async_copy(grad_out.at[part], grad_hbm.at[part], out_sem.at[2 + k]))
        late[k].start()

    for app in range(APPS):
        several = sent.at[app, pl.ds(0, TILES - 1)]
        pltpu.make_async_copy(several, several, send_sem.at[app]).wait()
    for copy in early + late:
        copy.wait()


def store(model, resid, grad, model_out, resid_out, grad_out, held, in_sem, out_sem):
    pairs = ((model, model_out), (resid, resid_out), (grad, grad_out))
    size = WIDTH // CHUNKS
    parts = [(k, j, pl.ds(j * size, size)) for k in range(3) for j in range(CHUNKS)]
    takes = [pltpu.make_async_copy(pairs[k][0].at[p], held.at[k, p], in_sem.at[k, j]) for k, j, p in parts]
    gives = [pltpu.make_async_copy(held.at[k, p], pairs[k][1].at[p], out_sem.at[k, j]) for k, j, p in parts]
    for take in takes:
        take.start()
    for take, give in zip(takes, gives):
        take.wait()
        give.start()
    for give in gives:
        give.wait()


def local(u_tiles, v_tiles, tile_ranks, recorded):
    rows = TILES * RANK
    field = jax.ShapeDtypeStruct((WIDTH, TRACES), jnp.float32)
    flat = pltpu.VMEM((TRACES, WIDTH), jnp.float32)
    hbm = pl.BlockSpec(memory_space=pltpu.HBM)
    outs = pl.pallas_call(
        kernel,
        out_shape=(field,) * 3,
        in_specs=[
            hbm,
            hbm,
            hbm,
            hbm,
        ],
        out_specs=(hbm,) * 3,
        scratch_shapes=[
            pltpu.VMEM((2, PLANE, NZ, RANK, WIDTH), jnp.bfloat16),
            pltpu.SMEM((TILES, TILES), jnp.int32),
            pltpu.VMEM((WIDTH, TRACES), jnp.float32),
            pltpu.VMEM((TRACES, WIDTH), jnp.bfloat16),
            flat, flat, flat, flat, flat,
            pltpu.VMEM((APPS, TILES, RANK, TRACES), jnp.bfloat16),
            pltpu.VMEM((APPS, TILES, RANK, TRACES), jnp.bfloat16),
            pltpu.VMEM((4, NZ, 1, 128), jnp.float32),
            pltpu.VMEM((4, NF, 1, 128), jnp.float32),
            pltpu.VMEM((4, PLANE, 1, 128), jnp.float32),
            pltpu.SemaphoreType.DMA((2, PLANE)),
            pltpu.SemaphoreType.DMA((2,)),
            pltpu.SemaphoreType.DMA((APPS,)),
            pltpu.SemaphoreType.DMA((APPS, PLANE)),
            pltpu.SemaphoreType.DMA((4, 3)),
            pltpu.SemaphoreType.DMA((4, 3)),
            pltpu.VMEM((WIDTH, TRACES), jnp.float32),
            pltpu.VMEM((WIDTH, TRACES), jnp.float32),
            pltpu.VMEM((WIDTH, TRACES), jnp.float32),
            pltpu.SemaphoreType.DMA((2 + CHUNKS,)),
            pltpu.SemaphoreType.REGULAR,
        ],
        compiler_params=pltpu.CompilerParams(
            collective_id=0, has_side_effects=True, vmem_limit_bytes=62 << 20
        ),
        cost_estimate=pl.CostEstimate(
            flops=APPS * 4 * rows * WIDTH * TRACES, bytes_accessed=12 << 20, transcendentals=0
        ),
    )(
        u_tiles.reshape(NZ, NX, NC, RANK, WIDTH),
        v_tiles.reshape(NZ, NX, NC, RANK, WIDTH),
        tile_ranks.reshape(TILES, TILES),
        recorded.reshape(WIDTH, TRACES),
    )
    outs = pl.pallas_call(
        store,
        out_shape=(field,) * 3,
        in_specs=[hbm] * 3,
        out_specs=(hbm,) * 3,
        scratch_shapes=[
            pltpu.VMEM((3, WIDTH, TRACES), jnp.float32),
            pltpu.SemaphoreType.DMA((3, CHUNKS)),
            pltpu.SemaphoreType.DMA((3, CHUNKS)),
        ],
    )(*outs)
    return tuple(out.reshape(1, WIDTH, TRACES) for out in outs)


def solution(mesh):
    torus = Mesh(mesh.devices.reshape(NZ, NX, NC, NF), ("z", "x", "c", "freq"))
    tile = ("z", "x", "c")
    in_specs = (
        P("freq", tile, None, None, None),
        P("freq", None, tile, None, None),
        P("freq", None, None),
        P("freq", tile, None),
    )
    out_specs = (P("freq", tile, None),) * 3
    return jax.shard_map(local, mesh=torus, in_specs=in_specs, out_specs=out_specs, check_vma=False)
```

```python
import jax
import jax.numpy as jnp
from jax import lax
from jax.experimental import pallas as pl
from jax.experimental.pallas import tpu as pltpu
from jax.sharding import Mesh
from jax.sharding import PartitionSpec as P

MESH = pl.DeviceIdType.MESH
NZ, NX, NC, NF = 8, 4, 2, 4
RANK, WIDTH, TRACES = 40, 1024, 128
PLANE = NX * NC
GROUP = NZ * RANK
TILES = NZ * PLANE
APPS = 5
CHUNKS = 4
PLANE_ORDER = ((2, 1), (2, 0), (1, 1), (3, 1), (1, 0), (3, 0), (0, 1), (0, 0))
ZONE_ORDER = (4, 3, 5, 2, 6, 1, 7, 0)


def kernel(
    u_hbm, v_hbm, ranks_hbm, recorded_hbm,
    model_hbm, resid_hbm, grad_hbm,
    w, ranks, recorded, field, total, resid, grad, image, direc,
    sent, held, red_a, red_b, red_c,
    load_sem, small_sem, send_sem, recv_sem,
    red_send, red_recv,
    model_out, resid_out, grad_out, out_sem, ready,
):
    z, x, c = lax.axis_index("z"), lax.axis_index("x"), lax.axis_index("c")
    freq = lax.axis_index("freq")
    place = x * NC + c
    me = z * PLANE + place
    mine = (c * NX + x) * NZ + z

    def across(step):
        half = (step + 1) // 2
        odd = lax.rem(step, 2)
        return lax.rem(NX // 2 + NX + (1 - 2 * odd) * half, NX)

    def offset_of(step):
        half = (step + 1) // 2
        odd = lax.rem(step, 2)
        return lax.rem(NZ // 2 + NZ + (1 - 2 * odd) * half, NZ)

    def at(dz, dx, dc):
        return {"z": lax.rem(z + dz, NZ), "x": lax.rem(x + dx, NX), "c": lax.rem(c + dc, NC)}

    def at_freq(df):
        return {"freq": lax.rem(freq + df, NF)}

    barrier = pltpu.get_barrier_semaphore()

    def greet(step, carry):
        for dx in (2, 1, 3, 0):
            pl.semaphore_signal(barrier, 1, device_id=at(offset_of(step), dx, 0), device_id_type=MESH)
        return carry

    lax.fori_loop(0, NZ - 1, greet, 0)
    for dx in (2, 1, 3):
        pl.semaphore_signal(barrier, 1, device_id=at(0, dx, 0), device_id_type=MESH)
    for df in range(1, NF):
        pl.semaphore_signal(barrier, 1, device_id=at_freq(df), device_id_type=MESH)

    def tell(semaphore):
        pl.semaphore_signal(semaphore, 1, device_id={"c": 1 - c}, device_id_type=MESH)

    pl.when(c == 1)(lambda: tell(barrier))

    def enter():
        pl.semaphore_wait(barrier, NZ * NX - 1 + NF - 1 + 1 - c)

    def ask():
        tell(ready)
        pl.semaphore_wait(ready, 1)

    def answer():
        pl.semaphore_wait(ready, 1)
        tell(ready)

    loads = [
        [
            pltpu.make_async_copy(
                hbm.at[:, part % NX, part // NX], w.at[k, part], load_sem.at[k, part]
            )
            for part in range(PLANE)
        ]
        for k, hbm in enumerate((u_hbm, v_hbm))
    ]
    small = [
        pltpu.make_async_copy(recorded_hbm, recorded, small_sem.at[0]),
        pltpu.make_async_copy(ranks_hbm, ranks, small_sem.at[1]),
    ]
    for parts in [small] + loads:
        for load in parts:
            load.start()

    def loaded(k):
        for load in loads[k]:
            load.wait()

    for load in small:
        load.wait()
    resid[...] = recorded[...].T
    field[...] = resid[...].astype(jnp.bfloat16)
    level = lax.broadcasted_iota(jnp.int32, (RANK, TRACES), 0)

    def partial_squares(value):
        return jnp.sum((value * value).reshape(TRACES // 8, 8, WIDTH // 128, 128), axis=(0, 2)).sum(axis=0, keepdims=True)

    def spread(s, which, count, slot, targets):
        buffer = (red_a, red_b, red_c)[which]
        for target in targets:
            pltpu.make_async_remote_copy(
                src_ref=buffer.at[s, slot],
                dst_ref=buffer.at[s, slot],
                send_sem=red_send.at[s, which],
                recv_sem=red_recv.at[s, which],
                device_id=target,
                device_id_type=MESH,
            ).start()

    def collect(s, which, count):
        buffer = (red_a, red_b, red_c)[which]
        several = buffer.at[s, pl.ds(0, count - 1)]
        pltpu.make_async_copy(several, several, red_recv.at[s, which]).wait()
        pltpu.make_async_copy(several, several, red_send.at[s, which]).wait()
        return jnp.sum(buffer[s], axis=0)

    def sum_first(s, value):
        red_a[s, z] = partial_squares(value)
        spread(s, 0, NZ, z, [at(dz, 0, 0) for dz in ZONE_ORDER if dz])

    def sum_second(s):
        red_b[s, freq] = collect(s, 0, NZ)
        spread(s, 1, NF, freq, [at_freq(df) for df in range(1, NF)])

    def sum_third(s):
        red_c[s, place] = collect(s, 1, NF)
        spread(s, 2, PLANE, place, [at(0, dx, dc) for dx, dc in PLANE_ORDER[:-1]])

    def sum_last(s):
        return jnp.sum(collect(s, 2, PLANE), keepdims=True)

    def apply(app, hooks=(None,) * 4):
        first = app % 2

        def coefficients(part):
            value = lax.dot_general(
                w[first, part].reshape(GROUP, WIDTH),
                field[...],
                (((1,), (1,)), ((), ())),
                preferred_element_type=jnp.float32,
            )
            for t in range(NZ):
                tile = t * PLANE + lax.rem(part, NX) * NC + part // NX
                rank = ranks[me, tile] if first == 0 else ranks[tile, me]
                rows = value[t * RANK : (t + 1) * RANK]
                sent[app, part * NZ + t] = jnp.where(level < rank, rows, 0.0).astype(jnp.bfloat16)

        def send(dz, part):
            slot = part * NZ + lax.rem(z + dz, NZ)
            pltpu.make_async_remote_copy(
                src_ref=sent.at[app, slot],
                dst_ref=held.at[app, mine],
                send_sem=send_sem.at[app],
                recv_sem=recv_sem.at[app, c * NX + x],
                device_id={"z": lax.rem(z + dz, NZ), "x": lax.rem(part, NX), "c": part // NX},
                device_id_type=MESH,
            ).start()

        def part_of(step, sign):
            dx = across(lax.rem(step, NX))
            return (1 - step // NX) * NX + lax.rem(x + sign * dx + NX, NX)

        def send_part(step, carry):
            part = part_of(step, 1)
            coefficients(part)
            if app == 0:
                pl.when(step == 0)(enter)
                pl.when((step == 0) & (c == 0))(ask)
                pl.when((step == NX) & (c == 1))(answer)
            for dz in ZONE_ORDER[:-1]:
                send(dz, part)
            pl.when(part != c * NX + x)(lambda: send(0, part))
            return carry

        def hook(k):
            if hooks[k] is not None:
                hooks[k]()

        hook(0)
        lax.fori_loop(0, 5, send_part, 0)
        hook(1)
        lax.fori_loop(5, PLANE, send_part, 0)
        own = pltpu.make_async_copy(sent.at[app, mine], held.at[app, mine], recv_sem.at[app, c * NX + x])
        own.start()

        total[...] = jnp.zeros_like(total)

        def take_part(step, carry):
            part = part_of(step, -1)
            start = pl.multiple_of(part * NZ, NZ)
            group = held.at[app, pl.ds(start, NZ)]
            pltpu.make_async_copy(group, group, recv_sem.at[app, part]).wait()
            value = held[app, pl.ds(start, NZ)].astype(jnp.float32)
            value = value.reshape(GROUP, TRACES).T.astype(jnp.bfloat16)
            total[...] += lax.dot_general(
                value,
                w[1 - first, part].reshape(GROUP, WIDTH),
                (((1,), (0,)), ((), ())),
                preferred_element_type=jnp.float32,
            )
            return carry

        lax.fori_loop(0, 1, take_part, 0)
        hook(2)
        lax.fori_loop(1, PLANE - 1, take_part, 0)
        hook(3)
        lax.fori_loop(PLANE - 1, PLANE, take_part, 0)

    def summing(k, value, late=None):
        return (
            lambda: sum_first(k, value[...]),
            lambda: sum_second(k),
            lambda: sum_third(k),
            late,
        )

    loaded(0)
    apply(0, (None, lambda: loaded(1), None, None))
    grad[...] = total[...]
    field[...] = grad[...].astype(jnp.bfloat16)
    apply(1, summing(0, grad))
    image[...] = total[...]
    field[...] = image[...].astype(jnp.bfloat16)
    apply(2, summing(1, image))
    gamma = sum_last(0)
    delta = sum_last(1)
    alpha = gamma / delta
    direc[...] = grad[...]
    grad[...] = grad[...] - alpha * total[...]
    field[...] = grad[...].astype(jnp.bfloat16)
    def step_resid():
        resid[...] = resid[...] - alpha * image[...]

    apply(3, summing(2, grad, step_resid))
    gamma_new = sum_last(2)
    beta = gamma_new / gamma
    image[...] = total[...] + beta * image[...]
    field[...] = image[...].astype(jnp.bfloat16)

    early = [
        pltpu.make_async_copy(value, hbm, out_sem.at[k])
        for k, (value, hbm) in enumerate(((model_out, model_hbm), (resid_out, resid_hbm)))
    ]

    def finish():
        scale = gamma_new / sum_last(3)
        old = direc[...]
        model_out[...] = (alpha * old + scale * (grad[...] + beta * old)).T
        resid_out[...] = (resid[...] - scale * image[...]).T
        direc[0:1, 0:128] = jnp.broadcast_to(scale, (1, 128))
        for copy in early:
            copy.start()

    apply(4, summing(3, image, finish))
    late = []
    for k in range(CHUNKS):
        part = pl.ds(k * WIDTH // CHUNKS, WIDTH // CHUNKS)
        grad_out[part] = (grad[:, part] - direc[0:1, 0:1] * total[:, part]).T
        late.append(pltpu.make_async_copy(grad_out.at[part], grad_hbm.at[part], out_sem.at[2 + k]))
        late[k].start()

    for app in range(APPS):
        several = sent.at[app, pl.ds(0, TILES - 1)]
        pltpu.make_async_copy(several, several, send_sem.at[app]).wait()
    for copy in early + late:
        copy.wait()


def store(model, resid, grad, model_out, resid_out, grad_out, held, in_sem, out_sem):
    pairs = ((model, model_out), (resid, resid_out), (grad, grad_out))
    size = WIDTH // CHUNKS
    parts = [(k, j, pl.ds(j * size, size)) for k in range(3) for j in range(CHUNKS)]
    takes = [pltpu.make_async_copy(pairs[k][0].at[p], held.at[k, p], in_sem.at[k, j]) for k, j, p in parts]
    gives = [pltpu.make_async_copy(held.at[k, p], pairs[k][1].at[p], out_sem.at[k, j]) for k, j, p in parts]
    for take in takes:
        take.start()
    for take, give in zip(takes, gives):
        take.wait()
        give.start()
    for give in gives:
        give.wait()


def local(u_tiles, v_tiles, tile_ranks, recorded):
    rows = TILES * RANK
    field = jax.ShapeDtypeStruct((WIDTH, TRACES), jnp.float32)
    flat = pltpu.VMEM((TRACES, WIDTH), jnp.float32)
    hbm = pl.BlockSpec(memory_space=pltpu.HBM)
    outs = pl.pallas_call(
        kernel,
        out_shape=(field,) * 3,
        in_specs=[
            hbm,
            hbm,
            hbm,
            hbm,
        ],
        out_specs=(hbm,) * 3,
        scratch_shapes=[
            pltpu.VMEM((2, PLANE, NZ, RANK, WIDTH), jnp.bfloat16),
            pltpu.SMEM((TILES, TILES), jnp.int32),
            pltpu.VMEM((WIDTH, TRACES), jnp.float32),
            pltpu.VMEM((TRACES, WIDTH), jnp.bfloat16),
            flat, flat, flat, flat, flat,
            pltpu.VMEM((APPS, TILES, RANK, TRACES), jnp.bfloat16),
            pltpu.VMEM((APPS, TILES, RANK, TRACES), jnp.bfloat16),
            pltpu.VMEM((4, NZ, 1, 128), jnp.float32),
            pltpu.VMEM((4, NF, 1, 128), jnp.float32),
            pltpu.VMEM((4, PLANE, 1, 128), jnp.float32),
            pltpu.SemaphoreType.DMA((2, PLANE)),
            pltpu.SemaphoreType.DMA((2,)),
            pltpu.SemaphoreType.DMA((APPS,)),
            pltpu.SemaphoreType.DMA((APPS, PLANE)),
            pltpu.SemaphoreType.DMA((4, 3)),
            pltpu.SemaphoreType.DMA((4, 3)),
            pltpu.VMEM((WIDTH, TRACES), jnp.float32),
            pltpu.VMEM((WIDTH, TRACES), jnp.float32),
            pltpu.VMEM((WIDTH, TRACES), jnp.float32),
            pltpu.SemaphoreType.DMA((2 + CHUNKS,)),
            pltpu.SemaphoreType.REGULAR,
        ],
        compiler_params=pltpu.CompilerParams(
            collective_id=0, has_side_effects=True, vmem_limit_bytes=62 << 20
        ),
        cost_estimate=pl.CostEstimate(
            flops=APPS * 4 * rows * WIDTH * TRACES, bytes_accessed=12 << 20, transcendentals=0
        ),
    )(
        u_tiles.reshape(NZ, NX, NC, RANK, WIDTH),
        v_tiles.reshape(NZ, NX, NC, RANK, WIDTH),
        tile_ranks.reshape(TILES, TILES),
        recorded.reshape(WIDTH, TRACES),
    )
    outs = pl.pallas_call(
        store,
        out_shape=(field,) * 3,
        in_specs=[hbm] * 3,
        out_specs=(hbm,) * 3,
        scratch_shapes=[
            pltpu.VMEM((3, WIDTH, TRACES), jnp.float32),
            pltpu.SemaphoreType.DMA((3, CHUNKS)),
            pltpu.SemaphoreType.DMA((3, CHUNKS)),
        ],
    )(*outs)
    return tuple(out.reshape(1, WIDTH, TRACES) for out in outs)


def solution(mesh):
    torus = Mesh(mesh.devices.reshape(NZ, NX, NC, NF), ("z", "x", "c", "freq"))
    tile = ("z", "x", "c")
    in_specs = (
        P("freq", tile, None, None, None),
        P("freq", None, tile, None, None),
        P("freq", None, None),
        P("freq", tile, None),
    )
    out_specs = (P("freq", tile, None),) * 3
    return jax.shard_map(local, mesh=torus, in_specs=in_specs, out_specs=out_specs, check_vma=False)
```
